32 devices in a mesh: blk: 8 (over y, x, core), grp: 4 (over z).
Axes of the slice: x: 2, y: 2, z: 4, core: 2. Of those that a mesh axis runs over, the one named last changes fastest.
Arguments:
- states: float32 [54, 16384], P(None, ('blk', 'grp')), may hold values from 0 to 1
- lengthscales: float32 [54], replicated, may hold values from 0.4 to 1
- noise_var: float32 [1], replicated, may hold values from 0.5 to 1.5
- solution: float32 [32, 16384], P(None, ('blk', 'grp')), may hold values from -6 to 6
- residual: float32 [32, 16384], P(None, ('blk', 'grp')), may hold values from -6 to 6, as said below
- direction: float32 [32, 16384], P(None, ('blk', 'grp')), may hold values from -6 to 6, as said below
Outputs:
- new_solution: float32 [32, 16384], P(None, ('blk', 'grp'))
- new_residual: float32 [32, 16384], P(None, ('blk', 'grp'))
- new_direction: float32 [32, 16384], P(None, ('blk', 'grp'))
The draws below stay inside these ranges and needn't reach their ends.
Inputs may be any that keep to these rules, and one draw needn't show every extreme that they name: `residual`: entries of order one. `direction`: entries of order one.
All inputs are finite; a program needn't handle non-finite values.
Results may differ from the reference program's by a relative error of at most 0.000071.
Values sent between devices are 32-bit elements; how exact they have to be, the bound alone decides.
A program may use at most 128 MiB of HBM per device.

```python
import math
import jax
import jax.numpy as jnp
from jax import lax

POINT_DIMENSION = 54
PROBES = 32
NPTS = 16384


def ramp_scale():
    return 0.5 + jnp.arange(NPTS, dtype=jnp.float32) / max(NPTS - 1, 1)


def draw_states(key, part):
    key = jax.random.fold_in(key, 5)
    keys = jax.random.split(key, 8)
    composition_fractions = jax.random.uniform(keys[0], (NPTS,), jnp.float32)
    chemical_conversion_extent = jax.random.uniform(keys[1], (NPTS,), jnp.float32)
    jitter = 0.03 * jax.random.truncated_normal(keys[2], -3.0, 3.0, (POINT_DIMENSION, NPTS), jnp.float32)
    amplitude = jax.random.uniform(keys[3], (POINT_DIMENSION, 1), jnp.float32, 0.15, 0.45)
    signs = jnp.where(jax.random.uniform(keys[4], (POINT_DIMENSION, 1), jnp.float32) < 0.5, -1.0, 1.0)
    freq_mixture = signs * jax.random.uniform(keys[5], (POINT_DIMENSION, 1), jnp.float32, 0.5, 2.0)
    freq_progress = jax.random.uniform(keys[6], (POINT_DIMENSION, 1), jnp.float32, 0.5, 2.0)
    phases = jax.random.uniform(keys[7], (POINT_DIMENSION, 1), jnp.float32, -math.pi, math.pi)
    angles = 2.0 * math.pi * (freq_mixture * composition_fractions[None, :] + freq_progress * chemical_conversion_extent[None, :]) + phases
    heat_distribution_curve = 0.5 + amplitude * jnp.cos(angles)
    kelvin_reading = 0.08 + 0.84 * chemical_conversion_extent[None, :] * (1.0 - 0.5 * jnp.abs(composition_fractions[None, :] - 0.5))
    heat_indicator = jnp.arange(POINT_DIMENSION)[:, None] == POINT_DIMENSION - 1
    heat_distribution_curve = jnp.where(heat_indicator, kelvin_reading, heat_distribution_curve)
    return jnp.clip(heat_distribution_curve + jitter, 0.0, 1.0)


def draw_residual(key, part):
    key = jax.random.fold_in(key, 11)
    values = jax.random.truncated_normal(key, -4.0, 4.0, (PROBES, NPTS), jnp.float32)
    return values * ramp_scale()[None, :]


def draw_direction(key, part):
    key = jax.random.fold_in(key, 23)
    values = jax.random.truncated_normal(key, -4.0, 4.0, (PROBES, NPTS), jnp.float32)
    return values * ramp_scale()[None, :]


def level_of(key, extent, shards, least, top_value):
    def one(position, shards_of):
        draws = jax.random.uniform(jax.random.fold_in(jax.random.fold_in(key, 6), position), (shards_of,), jnp.float32, least / len(shards), top_value / len(shards))
        return jnp.repeat(jnp.exp(draws), extent[position] // shards_of).reshape((-1,) + (1,) * (len(extent) - position - 1))

    loudness = one(*shards[0])
    for cut in shards[1:]:
        loudness = loudness * one(*cut)
    return loudness


def noise(own_key, dims, deviation, bound, cuts=(), held_as=jnp.bfloat16):
    entries = jax.random.normal(own_key, dims, jnp.float32) * deviation
    if len(cuts) > 0:
        entries = level_of(own_key, dims, cuts, -0.22, 0.18) * entries
    return jnp.clip(entries, min=-bound, max=bound).astype(held_as)


def setup_inputs(seed: int = 0) -> dict:
    key_list = jax.random.split(jax.random.key(seed), 7)
    states = draw_states(jax.random.fold_in(key_list[6], 71), 0)
    lengthscales = jnp.clip(jnp.exp(jax.random.uniform(key_list[1], (POINT_DIMENSION,), jnp.float32, math.log(0.4), math.log(1.0))), 0.4, 1.0)
    noise_var = jnp.clip(jax.random.uniform(key_list[2], (1,), jnp.float32, 0.5, 1.5), 0.5, 1.5)
    solution = noise(key_list[3], (PROBES, NPTS), 1.0, 6.0, ((1, 32),), jnp.float32)
    residual = draw_residual(jax.random.fold_in(key_list[6], 71), 0)
    direction = draw_direction(jax.random.fold_in(key_list[6], 71), 0)
    return dict(states=states, lengthscales=lengthscales, noise_var=noise_var, solution=solution, residual=residual, direction=direction)


def matern_tile(rows_scaled, row_norm, cols_scaled):
    cross_term = jnp.dot(rows_scaled.T, cols_scaled, precision=lax.Precision.HIGHEST, preferred_element_type=jnp.float32)
    column_norm_value = lax.optimization_barrier(jnp.sum(cols_scaled * cols_scaled, axis=0))
    sqdist = jnp.maximum(row_norm[:, None] + column_norm_value[None, :] - 2.0 * cross_term, 0.0)
    spread = jnp.sqrt(5.0 * sqdist)
    return (1.0 + spread + spread * spread / 3.0) * jnp.exp(-spread)

def reference(states, lengthscales, noise_var, solution, residual, direction):
    scaled = (states - 0.5) / lengthscales[:, None]
    norms = lax.optimization_barrier(jnp.sum(scaled * scaled, axis=0))
    row_width = math.gcd(NPTS, 1024)
    block_count = NPTS // row_width
    row_slabs = scaled.reshape(POINT_DIMENSION, block_count, row_width).transpose(1, 0, 2)
    norm_slabs = norms.reshape(block_count, row_width)

    def slab_image(pair):
        kernel = matern_tile(pair[0], pair[1], scaled)
        return lax.dot_general(direction, kernel, (((1,), (1,)), ((), ())), precision=lax.Precision.HIGHEST, preferred_element_type=jnp.float32)
    row_parts = lax.map(slab_image, (row_slabs, norm_slabs))
    image_sum = row_parts.transpose(1, 0, 2).reshape(PROBES, NPTS) + noise_var[0] * direction
    old_norm = lax.optimization_barrier(jnp.sum(residual * residual, axis=1))
    curvature = lax.optimization_barrier(jnp.sum(direction * image_sum, axis=1))
    step_size = old_norm / curvature
    new_solution = solution + step_size[:, None] * direction
    new_residual = residual - step_size[:, None] * image_sum
    new_norm = lax.optimization_barrier(jnp.sum(new_residual * new_residual, axis=1))
    new_direction = new_residual + (new_norm / old_norm)[:, None] * direction
    return (new_solution, new_residual, new_direction)
```

```python
import functools
import math

import jax
import jax.numpy as jnp
from jax import lax
from jax.experimental import pallas as pl
from jax.experimental.pallas import tpu as pltpu
from jax.sharding import PartitionSpec as P

MESH = pl.DeviceIdType.MESH
F32 = jnp.float32
BF16 = jnp.bfloat16
TO_T = math.sqrt(5.0) / math.log(2.0)
LN2 = math.log(2.0)


def partner(index, flip, count):
    bit = 1
    while bit < count:
        if not isinstance(flip, int):
            turn = lax.rem(lax.div(flip, bit), 2)
            index = index + turn * bit * (1 - 2 * lax.rem(lax.div(index, bit), 2))
        elif flip & bit:
            index = index + bit * (1 - 2 * lax.rem(lax.div(index, bit), 2))
        bit *= 2
    return index


def step_order(pairs, groups):
    order = [(p, r) for p in range(pairs - 1) for r in range(groups)]
    order.sort(key=lambda s: (max(s), s[0], s[1]))
    return order + [(pairs - 1, r) for r in reversed(range(groups))]


def split(x):
    high = x.astype(BF16).astype(F32)
    return high, (x - high).astype(BF16).astype(F32)


def norm_terms(high, low):
    both = high + low
    norm = jnp.sum(both * both, axis=0, keepdims=True)
    n1, rest = split(norm)
    n2 = rest
    n3 = (norm - n1 - n2).astype(BF16).astype(F32)
    return n1, n2, n3


def stacked(blocks, norms, first):
    width = blocks[0].shape[1]
    n1, n2, n3 = norms
    row = lax.broadcasted_iota(jnp.int32, (8, width), 0)
    at = first
    other = 3 - first
    extra = jnp.where((row >= other) & (row < other + 3), 1.0, 0.0)
    extra = jnp.where(row == at, n1, extra)
    extra = jnp.where(row == at + 1, n2, extra)
    extra = jnp.where(row == at + 2, n3, extra)
    used = sum(b.shape[0] for b in blocks) + 8
    depth = -(-used // 256) * 256
    parts = list(blocks) + [extra]
    if depth > used:
        parts.append(jnp.zeros((depth - used, width), F32))
    return jnp.concatenate(parts, axis=0)


def matern(x):
    x = jnp.maximum(x, 1e-30)
    t = x * lax.rsqrt(x)
    k = (x * (LN2 * LN2 / 3.0) + 1.0 + t * LN2) * jnp.exp2(-t)
    high = k.astype(BF16)
    return high, (k - high.astype(F32)).astype(BF16)


def kernel(
    nb, ng, dims, padded, st_ref, ls_ref, nv_ref, sol_ref, res_ref, dir_ref,
    nsol_ref, nres_ref, ndir_ref,
    colbuf, rowbuf, acol, brow, dd, acc, outbuf, redbuf, sums1, sums2,
    csend, crecv, fsend, frecv, rsend, rrecv, isend, irecv, s1send, s1recv, s2send, s2recv,
):
    b = lax.axis_index("blk")
    g = lax.axis_index("grp")
    pairs = nb // 2
    probes, n = dir_ref.shape
    q, core = lax.div(b, 2), lax.rem(b, 2)
    sibling = q * 2 + (1 - core)

    barrier = pltpu.get_barrier_semaphore()
    for k in range(1, nb):
        pl.semaphore_signal(barrier, inc=1, device_id=(partner(b, k, nb), g), device_id_type=MESH)
    for k in range(1, ng):
        pl.semaphore_signal(barrier, inc=1, device_id=(b, partner(g, k, ng)), device_id_type=MESH)

    colbuf[0, 0, padded - 8 : padded, :] = jnp.zeros((8, n), F32)
    colbuf[0, 0, 0:dims, :] = (st_ref[...] - 0.5) / ls_ref[...] * TO_T
    colbuf[0, 0, padded:, :] = dir_ref[...]
    acc[...] = jnp.zeros_like(acc)
    pl.semaphore_wait(barrier, nb + ng - 2)

    def direct(p):
        to = sibling if p is None else partner(q, p, pairs) * 2 + core
        slot = (0, 1) if p is None else (p, 0)
        at = 0 if p is None else p
        return pltpu.make_async_remote_copy(
            src_ref=colbuf.at[0, 0], dst_ref=colbuf.at[slot[0], slot[1]],
            send_sem=csend.at[at], recv_sem=crecv.at[at],
            device_id=(to, g), device_id_type=MESH,
        )

    def forward(p):
        return pltpu.make_async_remote_copy(
            src_ref=colbuf.at[p, 0], dst_ref=colbuf.at[p, 1],
            send_sem=fsend.at[p], recv_sem=frecv.at[p],
            device_id=(sibling, g), device_id_type=MESH,
        )

    def arrival(src, dst, sem):
        pltpu.make_async_copy(src, dst, sem).wait()

    def row_copy(r):
        return pltpu.make_async_remote_copy(
            src_ref=colbuf.at[0, 0, pl.ds(0, padded)], dst_ref=rowbuf.at[r],
            send_sem=rsend.at[r], recv_sem=rrecv.at[r],
            device_id=(b, partner(g, r, ng)), device_id_type=MESH,
        )

    def image_copy(r):
        return pltpu.make_async_remote_copy(
            src_ref=outbuf.at[r], dst_ref=redbuf.at[r],
            send_sem=isend.at[r], recv_sem=irecv.at[r],
            device_id=(b, partner(g, r, ng)), device_id_type=MESH,
        )

    direct(None).start()
    for k in range(1, max(pairs, ng)):
        if k < ng:
            row_copy(k).start()
        if k < pairs:
            direct(k).start()

    def prepare_rows(r, src):
        high, low = split(src)
        brow[r] = stacked([high, low, high, low], norm_terms(high, low), 3).astype(BF16)

    def prepare_columns(p, half):
        high, low = split(colbuf[p, half, 0:padded, :])
        left = stacked([-2.0 * high, -2.0 * high, -2.0 * low, -2.0 * low], norm_terms(high, low), 0)
        acol[p, half * n : (half + 1) * n, :] = left.T.astype(BF16)
        d1, d2 = split(colbuf[p, half, padded:, :])
        both = jnp.concatenate([d1, d2], axis=0).astype(BF16)
        dd[p, :, half * n : (half + 1) * n] = both
        dd[p, :, (2 + half) * n : (3 + half) * n] = both

    prepare_rows(0, colbuf[0, 0, 0:padded, :])

    order = step_order(pairs, ng)
    first_p, first_r, last_r = {}, {}, {}
    for s, (p, r) in enumerate(order):
        first_p.setdefault(p, s)
        first_r.setdefault(r, s)
        last_r[r] = s
    ahead = {}
    for p in range(1, pairs):
        s = max(first_p[p] - (1 if p == 1 else 2), 0)
        while s in ahead:
            s -= 1
        ahead[s] = p
    codes = []
    for s, (p, r) in enumerate(order):
        flags = (first_p[p] == s) + 2 * (first_r[r] == s and r > 0) + 4 * (last_r[r] == s and r > 0)
        codes.append(((ahead.get(s, 0) * 8 + flags) * ng + r) * pairs + p)

    def one_step(s, carry):
        code = jnp.int32(codes[0])
        for k in range(1, len(codes)):
            code = jnp.where(s == k, jnp.int32(codes[k]), code)
        p = lax.rem(code, pairs)
        r = lax.rem(lax.div(code, pairs), ng)
        flags = lax.rem(lax.div(code, pairs * ng), 8)
        early = lax.div(code, pairs * ng * 8)

        @pl.when(early > 0)
        def _():
            arrival(colbuf.at[0, 0], colbuf.at[early, 0], crecv.at[early])
            forward(early).start()

        @pl.when(lax.rem(flags, 2) == 1)
        def _():
            prepare_columns(p, 0)

            @pl.when(p == 0)
            def _():
                arrival(colbuf.at[0, 0], colbuf.at[0, 1], crecv.at[0])

            @pl.when(p > 0)
            def _():
                arrival(colbuf.at[0, 0], colbuf.at[p, 1], frecv.at[p])

            prepare_columns(p, 1)

        @pl.when(lax.rem(lax.div(flags, 2), 2) == 1)
        def _():
            arrival(colbuf.at[0, 0, pl.ds(0, padded)], rowbuf.at[r], rrecv.at[r])
            prepare_rows(r, rowbuf[r])

        x = jnp.dot(acol[p], brow[r], preferred_element_type=F32)
        high, low = matern(x)
        acc[r] += jnp.dot(dd[p], jnp.concatenate([high, low], axis=0), preferred_element_type=F32)

        @pl.when(flags >= 4)
        def _():
            outbuf[r] = acc[r, 0:probes, :] + acc[r, probes:, :]
            image_copy(r).start()

        return carry

    lax.fori_loop(0, len(codes), one_step, 0)

    direction = dir_ref[...]
    residual = res_ref[...]
    image = acc[0, 0:probes, :] + acc[0, probes:, :]
    for r in reversed(range(1, ng)):
        image_copy(r).wait_recv()
        image = image + redbuf[r]
    image = image + nv_ref[0, 0] * direction

    lane = lax.broadcasted_iota(jnp.int32, (128, 128), 1)
    gathered = jnp.zeros((128, 128), F32)
    for k, (u, v) in enumerate(
        [(residual, residual), (direction, image), (residual, image), (image, image)]
    ):
        one = jnp.sum(u * v, axis=1, keepdims=True)
        one = jnp.concatenate([one, jnp.zeros((128 - probes, 1), F32)], axis=0)
        gathered = jnp.where(lane == k, one, gathered)
    sums1[0] = gathered.T[0:8, :]

    def sums_copy(k, buf, send, recv, to):
        return pltpu.make_async_remote_copy(
            src_ref=buf.at[0], dst_ref=buf.at[k], send_sem=send.at[k], recv_sem=recv.at[k],
            device_id=to, device_id_type=MESH,
        )

    for k in range(1, nb):
        sums_copy(k, sums1, s1send, s1recv, (partner(b, k, nb), g)).start()
    total = sums1[0]
    for k in range(1, nb):
        sums_copy(k, sums1, s1send, s1recv, (partner(b, k, nb), g)).wait_recv()
        total = total + sums1[k]
    sums2[0] = total
    for k in range(1, ng):
        sums_copy(k, sums2, s2send, s2recv, (b, partner(g, k, ng))).start()
    for k in range(1, ng):
        sums_copy(k, sums2, s2send, s2recv, (b, partner(g, k, ng))).wait_recv()
        total = total + sums2[k]
    columns = jnp.concatenate([total, jnp.zeros((120, 128), F32)], axis=0).T
    rr, curv, ri, ii = [columns[0:probes, k : k + 1] for k in range(4)]
    alpha = rr / curv
    fresh = rr - 2.0 * alpha * ri + alpha * alpha * ii
    beta = fresh / rr
    nsol_ref[...] = sol_ref[...] + alpha * direction
    new_residual = residual - alpha * image
    nres_ref[...] = new_residual
    ndir_ref[...] = new_residual + beta * direction

    direct(None).wait_send()
    for k in range(1, pairs):
        direct(k).wait_send()
        forward(k).wait_send()
    for k in range(1, ng):
        row_copy(k).wait_send()
        image_copy(k).wait_send()
        sums_copy(k, sums2, s2send, s2recv, (b, partner(g, k, ng))).wait_send()
    for k in range(1, nb):
        sums_copy(k, sums1, s1send, s1recv, (partner(b, k, nb), g)).wait_send()


def solution(mesh):
    nb, ng = mesh.shape["blk"], mesh.shape["grp"]

    def per_device(states, lengthscales, noise_var, solution, residual, direction):
        dims, n = states.shape
        probes = direction.shape[0]
        padded = -(-dims // 8) * 8
        pairs = nb // 2
        depth = -(-(4 * padded + 8) // 256) * 256
        vmem = pl.BlockSpec(memory_space=pltpu.VMEM)
        smem = pl.BlockSpec(memory_space=pltpu.SMEM)
        dma = pltpu.SemaphoreType.DMA
        out = jax.ShapeDtypeStruct((probes, n), F32)
        return pl.pallas_call(
            functools.partial(kernel, nb, ng, dims, padded),
            out_shape=(out, out, out),
            in_specs=[vmem, vmem, smem, vmem, vmem, vmem],
            out_specs=(vmem, vmem, vmem),
            scratch_shapes=[
                pltpu.VMEM((pairs, 2, padded + probes, n), F32),
                pltpu.VMEM((ng, padded, n), F32),
                pltpu.VMEM((pairs, 2 * n, depth), BF16),
                pltpu.VMEM((ng, depth, n), BF16),
                pltpu.VMEM((pairs, 2 * probes, 4 * n), BF16),
                pltpu.VMEM((ng, 2 * probes, n), F32),
                pltpu.VMEM((ng, probes, n), F32),
                pltpu.VMEM((ng, probes, n), F32),
                pltpu.VMEM((nb, 8, 128), F32),
                pltpu.VMEM((ng, 8, 128), F32),
                dma((pairs,)), dma((pairs,)), dma((pairs,)), dma((pairs,)),
                dma((ng,)), dma((ng,)), dma((ng,)), dma((ng,)),
                dma((nb,)), dma((nb,)), dma((ng,)), dma((ng,)),
            ],
            compiler_params=pltpu.CompilerParams(
                collective_id=0, has_side_effects=True, vmem_limit_bytes=56 * 2**20
            ),
        )(states, lengthscales[:, None], noise_var[:, None], solution, residual, direction)

    spec = P(None, ("blk", "grp"))
    return jax.shard_map(
        per_device,
        mesh=mesh,
        in_specs=(spec, P(), P(), spec, spec, spec),
        out_specs=(spec, spec, spec),
        check_vma=False,
    )
```

```python
import functools
import math

import jax
import jax.numpy as jnp
from jax import lax
from jax.experimental import pallas as pl
from jax.experimental.pallas import tpu as pltpu
from jax.sharding import PartitionSpec as P

MESH = pl.DeviceIdType.MESH
F32 = jnp.float32
BF16 = jnp.bfloat16
TO_T = math.sqrt(5.0) / math.log(2.0)
LN2 = math.log(2.0)


def partner(index, flip, count):
    bit = 1
    while bit < count:
        if not isinstance(flip, int):
            turn = lax.rem(lax.div(flip, bit), 2)
            index = index + turn * bit * (1 - 2 * lax.rem(lax.div(index, bit), 2))
        elif flip & bit:
            index = index + bit * (1 - 2 * lax.rem(lax.div(index, bit), 2))
        bit *= 2
    return index


def step_order(pairs, groups):
    tail = [(p, 0) for p in range(max(pairs - 2, 1), pairs)]
    order = [(p, r) for p in range(pairs) for r in range(groups) if (p, r) not in tail]
    order.sort(key=lambda s: (max(2 * s[0], 4 * s[1] - 3), s[1], s[0]))
    return order + tail


def split(x):
    high = x.astype(BF16).astype(F32)
    return high, (x - high).astype(BF16).astype(F32)


def norm_terms(high, low):
    both = high + low
    norm = jnp.sum(both * both, axis=0, keepdims=True)
    n1, rest = split(norm)
    n2 = rest
    n3 = (norm - n1 - n2).astype(BF16).astype(F32)
    return n1, n2, n3


def stacked(blocks, norms, first):
    width = blocks[0].shape[1]
    n1, n2, n3 = norms
    row = lax.broadcasted_iota(jnp.int32, (8, width), 0)
    at = first
    other = 3 - first
    extra = jnp.where((row >= other) & (row < other + 3), 1.0, 0.0)
    extra = jnp.where(row == at, n1, extra)
    extra = jnp.where(row == at + 1, n2, extra)
    extra = jnp.where(row == at + 2, n3, extra)
    used = sum(b.shape[0] for b in blocks) + 8
    depth = -(-used // 256) * 256
    parts = list(blocks) + [extra]
    if depth > used:
        parts.append(jnp.zeros((depth - used, width), F32))
    return jnp.concatenate(parts, axis=0)


def matern(x):
    x = jnp.maximum(x, 1e-30)
    t = x * lax.rsqrt(x)
    k = (x * (LN2 * LN2 / 3.0) + 1.0 + t * LN2) * jnp.exp2(-t)
    high = k.astype(BF16)
    return high, (k - high.astype(F32)).astype(BF16)


def kernel(
    nb, ng, dims, padded, st_ref, ls_ref, nv_ref, res_ref, dir_ref,
    image_ref, steps_ref,
    colbuf, rowbuf, acol, brow, dd, acc, outbuf, redbuf, sums, xbuf,
    csend, crecv, fsend, frecv, rsend, rrecv, isend, irecv, ssend, srecv,
):
    b = lax.axis_index("blk")
    g = lax.axis_index("grp")
    pairs = nb // 2
    probes, n = dir_ref.shape
    q, core = lax.div(b, 2), lax.rem(b, 2)
    sibling = q * 2 + (1 - core)

    others = [(i, j) for i in range(nb) for j in range(ng) if i + j > 0]

    def other(i, j):
        return partner(b, i, nb), partner(g, j, ng)

    barrier = pltpu.get_barrier_semaphore()
    for i, j in others:
        pl.semaphore_signal(barrier, inc=1, device_id=other(i, j), device_id_type=MESH)

    diagonal = lax.broadcasted_iota(jnp.int32, (dims, dims), 0) == lax.broadcasted_iota(
        jnp.int32, (dims, dims), 1
    )
    lengths = jnp.sum(jnp.where(diagonal, ls_ref[...], 0.0), axis=1, keepdims=True)
    colbuf[0, 0, padded - 8 : padded, :] = jnp.zeros((8, n), F32)
    colbuf[0, 0, 0:dims, :] = (st_ref[...] - 0.5) / lengths * TO_T
    colbuf[0, 0, padded:, :] = dir_ref[...]
    acc[...] = jnp.zeros_like(acc)
    pl.semaphore_wait(barrier, len(others))

    def direct(p):
        to = sibling if p is None else partner(q, p, pairs) * 2 + core
        slot = (0, 1) if p is None else (p, 0)
        at = 0 if p is None else p
        return pltpu.make_async_remote_copy(
            src_ref=colbuf.at[0, 0], dst_ref=colbuf.at[slot[0], slot[1]],
            send_sem=csend.at[at], recv_sem=crecv.at[at],
            device_id=(to, g), device_id_type=MESH,
        )

    def forward(p):
        return pltpu.make_async_remote_copy(
            src_ref=colbuf.at[p, 0], dst_ref=colbuf.at[p, 1],
            send_sem=fsend.at[p], recv_sem=frecv.at[p],
            device_id=(sibling, g), device_id_type=MESH,
        )

    def arrival(src, dst, sem):
        pltpu.make_async_copy(src, dst, sem).wait()

    def row_copy(r):
        return pltpu.make_async_remote_copy(
            src_ref=colbuf.at[0, 0, pl.ds(0, padded)], dst_ref=rowbuf.at[r],
            send_sem=rsend.at[r], recv_sem=rrecv.at[r],
            device_id=(b, partner(g, r, ng)), device_id_type=MESH,
        )

    def image_copy(r):
        return pltpu.make_async_remote_copy(
            src_ref=outbuf.at[r], dst_ref=redbuf.at[r],
            send_sem=isend.at[r], recv_sem=irecv.at[r],
            device_id=(b, partner(g, r, ng)), device_id_type=MESH,
        )

    direct(None).start()
    if ng > 1:
        row_copy(1).start()
    for p in range(1, min(pairs, 3)):
        direct(p).start()

    def prepare_rows(r, src):
        high, low = split(src)
        brow[r] = stacked([high, low, high, low], norm_terms(high, low), 3).astype(BF16)

    def prepare_columns(p, half):
        high, low = split(colbuf[p, half, 0:padded, :])
        left = stacked([-2.0 * high, -2.0 * high, -2.0 * low, -2.0 * low], norm_terms(high, low), 0)
        acol[p, half * n : (half + 1) * n, :] = left.T.astype(BF16)
        d1, d2 = split(colbuf[p, half, padded:, :])
        both = jnp.concatenate([d1, d2], axis=0).astype(BF16)
        dd[p, :, half * n : (half + 1) * n] = both
        dd[p, :, (2 + half) * n : (3 + half) * n] = both

    order = step_order(pairs, ng)
    count = len(order)
    first_p, first_r, last_r = {}, {}, {}
    for s, (p, r) in enumerate(order):
        first_p.setdefault(p, s)
        first_r.setdefault(r, s)
        last_r[r] = s
    ahead = {}
    for p in range(3, pairs):
        s = first_p[p] - 2
        while s in ahead:
            s -= 1
        ahead[s] = p
    codes = []
    for s, (p, r) in enumerate(order):
        flags = (first_p[p] == s) + 2 * (first_r[r] == s) + 4 * (last_r[r] == s and r > 0)
        codes.append(((ahead.get(s, 0) * 8 + flags) * ng + r) * pairs + p)

    def decode(s):
        code = jnp.int32(codes[0])
        for k in range(1, count):
            code = jnp.where(s == k, jnp.int32(codes[k]), code)
        group = lax.div(code, pairs)
        flags = lax.div(group, ng)
        return lax.rem(code, pairs), lax.rem(group, ng), lax.rem(flags, 8), lax.div(flags, 8)

    def pass_on(p):
        arrival(colbuf.at[0, 0], colbuf.at[p, 0], crecv.at[p])
        forward(p).start()

    def rows_arrive(r):
        arrival(colbuf.at[0, 0, pl.ds(0, padded)], rowbuf.at[r], rrecv.at[r])
        prepare_rows(r, rowbuf[r])

    def columns_arrive(p):
        prepare_columns(p, 0)
        arrival(colbuf.at[0, 0], colbuf.at[p, 1], frecv.at[p])
        prepare_columns(p, 1)

    def get_ready(s):
        p, r, flags, early = decode(s)

        @pl.when(early > 0)
        def _():
            pass_on(early)

        @pl.when(lax.rem(flags, 2) == 1)
        def _():
            columns_arrive(p)

        @pl.when(lax.rem(lax.div(flags, 2), 2) == 1)
        def _():
            rows_arrive(r)

    def distance(p, r):
        return jnp.dot(acol[p], brow[r], preferred_element_type=F32)

    def accumulate(p, r, x):
        high, low = matern(x)
        acc[r] += jnp.dot(dd[p], jnp.concatenate([high, low], axis=0), preferred_element_type=F32)

    def send_off(r, flags):
        @pl.when(flags >= 4)
        def _():
            outbuf[r] = acc[r, 0:probes, :] + acc[r, probes:, :]
            image_copy(r).start()

    prepare_columns(0, 0)
    prepare_rows(0, colbuf[0, 0, 0:padded, :])
    arrival(colbuf.at[0, 0], colbuf.at[0, 1], crecv.at[0])
    prepare_columns(0, 1)
    xbuf[0] = distance(0, 0)
    seen = {("p", 0), ("r", 0)}
    for s in range(1, 3):
        p, r = order[s]
        if ("r", r) not in seen:
            rows_arrive(r)
            if r + 1 < ng:
                row_copy(r + 1).start()
        if ("p", p) not in seen:
            for k in range(1, min(pairs, 3)):
                pass_on(k)
            if pairs > 3:
                direct(3).start()
            columns_arrive(p)
        seen |= {("p", p), ("r", r)}

    def two_steps(i, carry):
        s = 2 * i
        p0, r0, flags0, _ = decode(s)
        p1, r1, flags1, _ = decode(s + 1)
        p2, r2, _, _ = decode(s + 2)
        xbuf[1] = distance(p1, r1)
        accumulate(p0, r0, xbuf[0])
        xbuf[0] = distance(p2, r2)
        accumulate(p1, r1, xbuf[1])
        send_off(r0, flags0)
        send_off(r1, flags1)
        for first, total, copy in ((3, ng, row_copy), (4, pairs, direct)):
            if first < total:

                @pl.when(i + first < total)
                def _():
                    copy(i + first).start()

        def ready(k, carry):
            get_ready(s + 3 + k)
            return carry

        lax.fori_loop(0, jnp.minimum(2, count - 3 - s), ready, 0)
        return carry

    lax.fori_loop(0, count // 2 - 1, two_steps, 0)
    (p0, r0), (p1, r1) = order[-2:]
    xbuf[1] = distance(p1, r1)
    accumulate(p0, r0, xbuf[0])
    accumulate(p1, r1, xbuf[1])

    direction = dir_ref[...]
    residual = res_ref[...]
    image = acc[0, 0:probes, :] + acc[0, probes:, :]
    for r in reversed(range(1, ng)):
        image_copy(r).wait_recv()
        image = image + redbuf[r]
    image = image + nv_ref[0, 0] * direction

    products = [residual * residual, direction * image, residual * image, image * image]
    columns = jnp.concatenate([jnp.sum(u, axis=1, keepdims=True) for u in products], axis=0)
    sums[0] = jnp.broadcast_to(columns, (4 * probes, 128)).T[0:1, :]

    def sums_copy(i, j):
        slot = i * ng + j
        return pltpu.make_async_remote_copy(
            src_ref=sums.at[0], dst_ref=sums.at[slot], send_sem=ssend.at[slot], recv_sem=srecv.at[slot],
            device_id=other(i, j), device_id_type=MESH,
        )

    for i, j in others:
        sums_copy(i, j).start()
    image_ref[...] = image
    for i, j in others:
        sums_copy(i, j).wait_recv()
    total = jnp.sum(sums[...], axis=0)
    totals = jnp.broadcast_to(total, (128, 4 * probes)).T
    rr, curv, ri, ii = [totals[k * probes : (k + 1) * probes, :] for k in range(4)]
    alpha = rr / curv
    fresh = rr - 2.0 * alpha * ri + alpha * alpha * ii
    steps_ref[0] = alpha
    steps_ref[1] = fresh / rr

    direct(None).wait_send()
    for k in range(1, pairs):
        direct(k).wait_send()
        forward(k).wait_send()
    for k in range(1, ng):
        row_copy(k).wait_send()
        image_copy(k).wait_send()
    for i, j in others:
        sums_copy(i, j).wait_send()


def solution(mesh):
    nb, ng = mesh.shape["blk"], mesh.shape["grp"]

    def per_device(states, lengthscales, noise_var, solution, residual, direction):
        dims, n = states.shape
        probes = direction.shape[0]
        padded = -(-dims // 8) * 8
        pairs = nb // 2
        depth = -(-(4 * padded + 8) // 256) * 256
        vmem = pl.BlockSpec(memory_space=pltpu.VMEM)
        smem = pl.BlockSpec(memory_space=pltpu.SMEM)
        dma = pltpu.SemaphoreType.DMA
        image, steps = pl.pallas_call(
            functools.partial(kernel, nb, ng, dims, padded),
            out_shape=(
                jax.ShapeDtypeStruct((probes, n), F32),
                jax.ShapeDtypeStruct((2, probes, 128), F32),
            ),
            in_specs=[vmem, vmem, smem, vmem, vmem],
            out_specs=(vmem, vmem),
            scratch_shapes=[
                pltpu.VMEM((pairs, 2, padded + probes, n), F32),
                pltpu.VMEM((ng, padded, n), F32),
                pltpu.VMEM((pairs, 2 * n, depth), BF16),
                pltpu.VMEM((ng, depth, n), BF16),
                pltpu.VMEM((pairs, 2 * probes, 4 * n), BF16),
                pltpu.VMEM((ng, 2 * probes, n), F32),
                pltpu.VMEM((ng, probes, n), F32),
                pltpu.VMEM((ng, probes, n), F32),
                pltpu.VMEM((nb * ng, 1, 4 * probes), F32),
                pltpu.VMEM((2, 2 * n, n), F32),
                dma((pairs,)), dma((pairs,)), dma((pairs,)), dma((pairs,)),
                dma((ng,)), dma((ng,)), dma((ng,)), dma((ng,)),
                dma((nb * ng,)), dma((nb * ng,)),
            ],
            compiler_params=pltpu.CompilerParams(
                collective_id=0, has_side_effects=True, vmem_limit_bytes=56 * 2**20
            ),
        )(states, lengthscales[None, :], noise_var[:, None], residual, direction)
        alpha, beta = steps[0, :, 0:1], steps[1, :, 0:1]
        new_residual = residual - alpha * image
        return solution + alpha * direction, new_residual, new_residual + beta * direction

    spec = P(None, ("blk", "grp"))
    return jax.shard_map(
        per_device,
        mesh=mesh,
        in_specs=(spec, P(), P(), spec, spec, spec),
        out_specs=(spec, spec, spec),
        check_vma=False,
    )
```

```python
import functools
import math

import jax
import jax.numpy as jnp
from jax import lax
from jax.experimental import pallas as pl
from jax.experimental.pallas import tpu as pltpu
from jax.sharding import PartitionSpec as P

MESH = pl.DeviceIdType.MESH
F32 = jnp.float32
BF16 = jnp.bfloat16
TO_T = math.sqrt(5.0) / math.log(2.0)
LN2 = math.log(2.0)


def partner(index, flip, count):
    bit = 1
    while bit < count:
        if not isinstance(flip, int):
            turn = lax.rem(lax.div(flip, bit), 2)
            index = index + turn * bit * (1 - 2 * lax.rem(lax.div(index, bit), 2))
        elif flip & bit:
            index = index + bit * (1 - 2 * lax.rem(lax.div(index, bit), 2))
        bit *= 2
    return index


def step_order(pairs, groups):
    tail = [(p, 0) for p in range(max(pairs - 2, 1), pairs)]
    order = [(p, r) for p in range(pairs) for r in range(groups) if (p, r) not in tail]
    order.sort(key=lambda s: (max(2 * s[0], 4 * s[1] - 3), s[1], s[0]))
    return order + tail


def split(x):
    high = x.astype(BF16).astype(F32)
    return high, (x - high).astype(BF16).astype(F32)


def norm_terms(high, low):
    both = high + low
    norm = jnp.sum(both * both, axis=0, keepdims=True)
    n1, rest = split(norm)
    n2 = rest
    n3 = (norm - n1 - n2).astype(BF16).astype(F32)
    return n1, n2, n3


def stacked(blocks, norms, first):
    width = blocks[0].shape[1]
    n1, n2, n3 = norms
    row = lax.broadcasted_iota(jnp.int32, (8, width), 0)
    at = first
    other = 3 - first
    extra = jnp.where((row >= other) & (row < other + 3), 1.0, 0.0)
    extra = jnp.where(row == at, n1, extra)
    extra = jnp.where(row == at + 1, n2, extra)
    extra = jnp.where(row == at + 2, n3, extra)
    used = sum(b.shape[0] for b in blocks) + 8
    depth = -(-used // 256) * 256
    parts = list(blocks) + [extra]
    if depth > used:
        parts.append(jnp.zeros((depth - used, width), F32))
    return jnp.concatenate(parts, axis=0)


def matern(x):
    x = jnp.maximum(x, 1e-30)
    t = x * lax.rsqrt(x)
    k = (x * (LN2 * LN2 / 3.0) + 1.0 + t * LN2) * jnp.exp2(-t)
    high = k.astype(BF16)
    return high, (k - high.astype(F32)).astype(BF16)


def kernel(
    nb, ng, dims, padded, st_ref, ls_ref, nv_ref, res_ref, dir_ref,
    image_ref, alpha_ref, beta_ref,
    colbuf, rowbuf, acol, brow, dd, acc, outbuf, redbuf, sums, xbuf,
    csend, crecv, fsend, frecv, rsend, rrecv, isend, irecv, ssend, srecv,
):
    b = lax.axis_index("blk")
    g = lax.axis_index("grp")
    pairs = nb // 2
    probes, n = dir_ref.shape
    q, core = lax.div(b, 2), lax.rem(b, 2)
    sibling = q * 2 + (1 - core)

    others = [(i, j) for i in range(nb) for j in range(ng) if i + j > 0]

    def other(i, j):
        return partner(b, i, nb), partner(g, j, ng)

    barrier = pltpu.get_barrier_semaphore()
    for i, j in others:
        pl.semaphore_signal(barrier, inc=1, device_id=other(i, j), device_id_type=MESH)

    diagonal = lax.broadcasted_iota(jnp.int32, (dims, dims), 0) == lax.broadcasted_iota(
        jnp.int32, (dims, dims), 1
    )
    lengths = jnp.sum(jnp.where(diagonal, ls_ref[...], 0.0), axis=1, keepdims=True)
    colbuf[0, 0, padded - 8 : padded, :] = jnp.zeros((8, n), F32)
    colbuf[0, 0, 0:dims, :] = (st_ref[...] - 0.5) / lengths * TO_T
    colbuf[0, 0, padded:, :] = dir_ref[...]
    acc[...] = jnp.zeros_like(acc)

    def direct(p):
        to = sibling if p is None else partner(q, p, pairs) * 2 + core
        slot = (0, 1) if p is None else (p, 0)
        at = 0 if p is None else p
        return pltpu.make_async_remote_copy(
            src_ref=colbuf.at[0, 0], dst_ref=colbuf.at[slot[0], slot[1]],
            send_sem=csend.at[at], recv_sem=crecv.at[at],
            device_id=(to, g), device_id_type=MESH,
        )

    def forward(p):
        return pltpu.make_async_remote_copy(
            src_ref=colbuf.at[p, 0], dst_ref=colbuf.at[p, 1],
            send_sem=fsend.at[p], recv_sem=frecv.at[p],
            device_id=(sibling, g), device_id_type=MESH,
        )

    def arrival(src, dst, sem):
        pltpu.make_async_copy(src, dst, sem).wait()

    def row_copy(r):
        return pltpu.make_async_remote_copy(
            src_ref=colbuf.at[0, 0, pl.ds(0, padded)], dst_ref=rowbuf.at[r],
            send_sem=rsend.at[r], recv_sem=rrecv.at[r],
            device_id=(b, partner(g, r, ng)), device_id_type=MESH,
        )

    def image_copy(r):
        return pltpu.make_async_remote_copy(
            src_ref=outbuf.at[r], dst_ref=redbuf.at[r],
            send_sem=isend.at[r], recv_sem=irecv.at[r],
            device_id=(b, partner(g, r, ng)), device_id_type=MESH,
        )

    def prepare_rows(r, src):
        high, low = split(src)
        brow[r] = stacked([high, low, high, low], norm_terms(high, low), 3).astype(BF16)

    def prepare_columns(p, half):
        high, low = split(colbuf[p, half, 0:padded, :])
        left = stacked([-2.0 * high, -2.0 * high, -2.0 * low, -2.0 * low], norm_terms(high, low), 0)
        acol[p, half * n : (half + 1) * n, :] = left.T.astype(BF16)
        d1, d2 = split(colbuf[p, half, padded:, :])
        both = jnp.concatenate([d1, d2], axis=0).astype(BF16)
        dd[p, :, half * n : (half + 1) * n] = both
        dd[p, :, (2 + half) * n : (3 + half) * n] = both

    order = step_order(pairs, ng)
    count = len(order)
    first_p, first_r, last_r = {}, {}, {}
    for s, (p, r) in enumerate(order):
        first_p.setdefault(p, s)
        first_r.setdefault(r, s)
        last_r[r] = s
    ahead = {}
    for p in range(3, pairs):
        s = first_p[p] - 2
        while s in ahead:
            s -= 1
        ahead[s] = p
    codes = []
    for s, (p, r) in enumerate(order):
        flags = (first_p[p] == s) + 2 * (first_r[r] == s) + 4 * (last_r[r] == s and r > 0)
        codes.append(((ahead.get(s, 0) * 8 + flags) * ng + r) * pairs + p)

    def decode(s):
        code = jnp.int32(codes[0])
        for k in range(1, count):
            code = jnp.where(s == k, jnp.int32(codes[k]), code)
        group = lax.div(code, pairs)
        flags = lax.div(group, ng)
        return lax.rem(code, pairs), lax.rem(group, ng), lax.rem(flags, 8), lax.div(flags, 8)

    def pass_on(p):
        arrival(colbuf.at[0, 0], colbuf.at[p, 0], crecv.at[p])
        forward(p).start()

    def rows_arrive(r):
        arrival(colbuf.at[0, 0, pl.ds(0, padded)], rowbuf.at[r], rrecv.at[r])
        prepare_rows(r, rowbuf[r])

    def columns_arrive(p):
        prepare_columns(p, 0)
        arrival(colbuf.at[0, 0], colbuf.at[p, 1], frecv.at[p])
        prepare_columns(p, 1)

    def get_ready(s):
        p, r, flags, early = decode(s)

        @pl.when(early > 0)
        def _():
            pass_on(early)

        @pl.when(lax.rem(flags, 2) == 1)
        def _():
            columns_arrive(p)

        @pl.when(lax.rem(lax.div(flags, 2), 2) == 1)
        def _():
            rows_arrive(r)

    def distance(p, r):
        return jnp.dot(acol[p], brow[r], preferred_element_type=F32)

    def accumulate(p, r, x):
        high, low = matern(x)
        acc[r] += jnp.dot(dd[p], jnp.concatenate([high, low], axis=0), preferred_element_type=F32)

    def send_off(r, flags):
        @pl.when(flags >= 4)
        def _():
            outbuf[r] = acc[r, 0:probes, :] + acc[r, probes:, :]
            image_copy(r).start()

    pl.semaphore_wait(barrier, len(others))
    direct(None).start()
    if ng > 1:
        row_copy(1).start()
    for p in range(1, min(pairs, 3)):
        direct(p).start()

    prepare_columns(0, 0)
    prepare_rows(0, colbuf[0, 0, 0:padded, :])
    arrival(colbuf.at[0, 0], colbuf.at[0, 1], crecv.at[0])
    prepare_columns(0, 1)
    accumulate(0, 0, distance(0, 0))
    rows_arrive(1)
    if ng > 2:
        row_copy(2).start()
    accumulate(0, 1, distance(0, 1))
    for k in range(1, min(pairs, 3)):
        pass_on(k)
    if pairs > 3:
        direct(3).start()
    columns_arrive(1)
    xbuf[0] = distance(1, 0)
    columns_arrive(2)

    def two_steps(i, carry):
        s = 2 * i
        p0, r0, flags0, _ = decode(s)
        p1, r1, flags1, _ = decode(s + 1)
        p2, r2, _, _ = decode(s + 2)
        xbuf[1] = distance(p1, r1)
        accumulate(p0, r0, xbuf[0])
        xbuf[0] = distance(p2, r2)
        accumulate(p1, r1, xbuf[1])
        send_off(r0, flags0)
        send_off(r1, flags1)
        for first, total, copy in ((2, ng, row_copy), (3, pairs, direct)):
            if first < total:

                @pl.when(i + first < total)
                def _():
                    copy(i + first).start()

        def ready(k, carry):
            get_ready(s + 3 + k)
            return carry

        lax.fori_loop(0, jnp.minimum(2, count - 3 - s), ready, 0)
        return carry

    lax.fori_loop(1, count // 2 - 1, two_steps, 0)
    (p0, r0), (p1, r1) = order[-2:]
    xbuf[1] = distance(p1, r1)
    accumulate(p0, r0, xbuf[0])
    accumulate(p1, r1, xbuf[1])

    direction = dir_ref[...]
    residual = res_ref[...]
    image = acc[0, 0:probes, :] + acc[0, probes:, :]
    for r in reversed(range(1, ng)):
        image_copy(r).wait_recv()
        image = image + redbuf[r]
    image = image + nv_ref[0, 0] * direction

    products = [residual * residual, direction * image, residual * image, image * image]
    columns = jnp.concatenate([jnp.sum(u, axis=1, keepdims=True) for u in products], axis=0)
    sums[0] = jnp.broadcast_to(columns, (4 * probes, 128)).T[0:1, :]

    def sums_copy(i, j):
        slot = i * ng + j
        return pltpu.make_async_remote_copy(
            src_ref=sums.at[0], dst_ref=sums.at[slot], send_sem=ssend.at[slot], recv_sem=srecv.at[slot],
            device_id=other(i, j), device_id_type=MESH,
        )

    for i, j in others:
        sums_copy(i, j).start()
    image_ref[...] = image
    for i, j in others:
        sums_copy(i, j).wait_recv()
    total = jnp.sum(sums[...], axis=0)
    totals = jnp.broadcast_to(total, (128, 4 * probes)).T
    rr, curv, ri, ii = [totals[k * probes : (k + 1) * probes, :] for k in range(4)]
    alpha = rr / curv
    fresh = rr - 2.0 * alpha * ri + alpha * alpha * ii
    beta = fresh / rr
    for k in range(n // 128):
        alpha_ref[:, k * 128 : (k + 1) * 128] = alpha
        beta_ref[:, k * 128 : (k + 1) * 128] = beta

    direct(None).wait_send()
    for k in range(1, pairs):
        direct(k).wait_send()
        forward(k).wait_send()
    for k in range(1, ng):
        row_copy(k).wait_send()
        image_copy(k).wait_send()
    for i, j in others:
        sums_copy(i, j).wait_send()


def solution(mesh):
    nb, ng = mesh.shape["blk"], mesh.shape["grp"]

    def per_device(states, lengthscales, noise_var, solution, residual, direction):
        dims, n = states.shape
        probes = direction.shape[0]
        padded = -(-dims // 8) * 8
        pairs = nb // 2
        depth = -(-(4 * padded + 8) // 256) * 256
        vmem = pl.BlockSpec(memory_space=pltpu.VMEM)
        smem = pl.BlockSpec(memory_space=pltpu.SMEM)
        dma = pltpu.SemaphoreType.DMA
        image, alpha, beta = pl.pallas_call(
            functools.partial(kernel, nb, ng, dims, padded),
            out_shape=(
                jax.ShapeDtypeStruct((probes, n), F32),
                jax.ShapeDtypeStruct((probes, n), F32),
                jax.ShapeDtypeStruct((probes, n), F32),
            ),
            in_specs=[vmem, vmem, smem, vmem, vmem],
            out_specs=(vmem, vmem, vmem),
            scratch_shapes=[
                pltpu.VMEM((pairs, 2, padded + probes, n), F32),
                pltpu.VMEM((ng, padded, n), F32),
                pltpu.VMEM((pairs, 2 * n, depth), BF16),
                pltpu.VMEM((ng, depth, n), BF16),
                pltpu.VMEM((pairs, 2 * probes, 4 * n), BF16),
                pltpu.VMEM((ng, 2 * probes, n), F32),
                pltpu.VMEM((ng, probes, n), F32),
                pltpu.VMEM((ng, probes, n), F32),
                pltpu.VMEM((nb * ng, 1, 4 * probes), F32),
                pltpu.VMEM((2, 2 * n, n), F32),
                dma((pairs,)), dma((pairs,)), dma((pairs,)), dma((pairs,)),
                dma((ng,)), dma((ng,)), dma((ng,)), dma((ng,)),
                dma((nb * ng,)), dma((nb * ng,)),
            ],
            compiler_params=pltpu.CompilerParams(
                collective_id=0, has_side_effects=True, vmem_limit_bytes=56 * 2**20
            ),
        )(states, lengthscales[None, :], noise_var[:, None], residual, direction)
        new_residual = residual - alpha * image
        return solution + alpha * direction, new_residual, new_residual + beta * direction

    spec = P(None, ("blk", "grp"))
    return jax.shard_map(
        per_device,
        mesh=mesh,
        in_specs=(spec, P(), P(), spec, spec, spec),
        out_specs=(spec, spec, spec),
        check_vma=False,
    )
```
